32 devices in a mesh: phase: 8 (over z, y), sect: 4 (over x, core).
Axes of the slice: x: 2, y: 2, z: 4, core: 2. Of those that a mesh axis runs over, the one named last changes fastest.
Arguments:
- activations: bfloat16 [1024, 32768], P('phase', 'sect'), may hold values from 0 to 2
- block_tiles: bfloat16 [8, 512, 8, 4096], P('phase', 'sect'), may hold values from -0.25 to 0.25
- sources: int32 [8, 512, 8], P('phase', 'sect'), may hold values from 0 to 511, all different within a row
- layer_bias: float32 [8], P('phase'), may hold values from -0.6 to -0.2
Outputs:
- next_acts: bfloat16 [1024, 32768], P('phase', 'sect')
The draws below stay inside these ranges and needn't reach their ends.
Inputs may be any that keep to these rules, and one draw needn't show every extreme that they name: `sources`: each row of 8 entries names distinct input blocks.
All inputs are finite; a program needn't handle non-finite values.
Results may differ from the reference program's by a relative error of at most 0.0055.
Values may be sent and summed in bfloat16 or wider, within the bound.
No kernel may reach another device: no remote copies, remote signals or barrier semaphores. Data moves between devices by JAX's collectives and lax.ppermute only.
A program may use at most 128 MiB of HBM per device.

```python
import jax
import jax.numpy as jnp
from jax import lax

NEUR = 32768
BLK = 64
FANIN = 8
ROWS = 128
TICKS = 2
LAYERS = 8
NB = 512
IMAGES = 1024


def level_of(own_key, extent, split, low, largest):
    def one(dim, blocks):
        steps = jax.random.uniform(jax.random.fold_in(jax.random.fold_in(own_key, 6), dim), (blocks,), jnp.float32, low / len(split), largest / len(split))
        return jnp.repeat(jnp.exp(steps), extent[dim] // blocks).reshape((-1,) + (1,) * (len(extent) - dim - 1))

    loudness = one(*split[0])
    for cut in split[1:]:
        loudness = loudness * one(*cut)
    return loudness


def picks_of(key, rows, number_of, top, lift):
    order = jax.random.permutation(jax.random.fold_in(key, 1), number_of)
    boost = order
    for power in range(3):
        boost = boost * boost // number_of
    boost = boost * lift // number_of
    lots = jax.random.randint(jax.random.fold_in(key, 2), (rows, number_of), 0, 4096) + boost
    holders = jax.random.permutation(jax.random.fold_in(key, 3), rows)[jnp.arange(number_of) % rows]
    lots = jnp.where(jnp.arange(rows)[:, None] == holders[None, :], 1 << 14, lots)
    priority = lots * number_of + jnp.arange(number_of)
    return lax.top_k(priority.astype(jnp.int32), top)[1].astype(jnp.int32)


def normal_values(rng, extent, deviation, reach, split=(), kind=jnp.bfloat16):
    result = jax.random.normal(rng, extent, jnp.float32) * deviation
    if len(split) > 0:
        result = level_of(rng, extent, split, -0.22, 0.18) * result
    return jnp.clip(result, min=-reach, max=reach).astype(kind)


def setup_inputs(seed: int = 0) -> dict:
    splits = jax.random.split(jax.random.key(seed), 5)
    return {
        "activations": jnp.clip(2.0 * jax.random.uniform(splits[0], (IMAGES, NEUR), jnp.float32) ** level_of(splits[0], (IMAGES, NEUR), ((0, 8), (1, 4)), -0.2, 0.2), 0.0, 2.0).astype(jnp.bfloat16),
        "block_tiles": normal_values(splits[1], (LAYERS, NB, FANIN, BLK * BLK), (FANIN * BLK) ** -0.5, 0.25, ((0, 8), (1, 4))),
        "sources": picks_of(splits[2], LAYERS * NB, NB, FANIN, 256).reshape((LAYERS, NB, FANIN)),
        "layer_bias": jnp.clip(-0.6 + 0.400000021 * jax.random.uniform(splits[3], (LAYERS,), jnp.float32) ** level_of(splits[3], (LAYERS,), ((0, 8),), -0.2, 0.2), -0.6, -0.2),
    }


def layer_output(state_rows, tiles_layer, sources_layer, bias_value):
    blocks = state_rows.astype(jnp.float32).reshape(ROWS, NB, BLK)
    picked = jnp.take(blocks, sources_layer, axis=1)
    weights = tiles_layer.astype(jnp.float32).reshape(NB, FANIN, BLK, BLK)
    summed = jnp.einsum("rjki,jkio->rjo", picked, weights)
    return jax.nn.relu(summed.reshape(ROWS, NEUR) + bias_value).astype(jnp.bfloat16)


def reference(activations, block_tiles, sources, layer_bias):
    state = activations.reshape(LAYERS, ROWS, NEUR)
    for tick_index in range(TICKS):
        hidden = lax.map(lambda packed: layer_output(*packed), (state, block_tiles, sources, layer_bias))
        state = jnp.roll(hidden, 1, axis=0)
    return state.reshape(LAYERS * ROWS, NEUR)
```

```python
import functools

import jax
import jax.numpy as jnp
from jax import lax
from jax.experimental import pallas as pl
from jax.experimental.pallas import tpu as pltpu
from jax.sharding import PartitionSpec as P

BLK = 64
LANES = 128
WIDE = 4
CHUNKS = (32, 32, 32, 32)
MIB = 1 << 20


def arrange_body(groups, tiles_ref, out_ref, order_ref):
    fanin = tiles_ref.shape[1]
    depth = fanin * BLK
    half = depth // 2

    @pl.when(pl.program_id(0) == 0)
    def _():
        row = lax.broadcasted_iota(jnp.int32, (depth, depth), 0)
        column = lax.broadcasted_iota(jnp.int32, (depth, depth), 1)
        neuron = row % BLK
        origin = (neuron % 2) * half + (neuron // 2) * fanin + row // BLK
        order_ref[...] = jnp.where(column == origin, 1.0, 0.0).astype(jnp.bfloat16)

    low = lax.broadcasted_iota(jnp.int32, (half, LANES), 1) < BLK
    for group in range(groups):
        stacked = []
        for member in range(WIDE):
            flat = tiles_ref[group * WIDE + member].astype(jnp.float32)
            stacked.append(jnp.concatenate([flat[:, t * LANES:(t + 1) * LANES] for t in range(half // fanin)], axis=0))
        even, odd = [], []
        for pair in range(WIDE // 2):
            first, second = stacked[2 * pair], stacked[2 * pair + 1]
            even.append(jnp.where(low, first, pltpu.roll(second, BLK, axis=1)).astype(jnp.bfloat16))
            odd.append(jnp.where(low, pltpu.roll(first, BLK, axis=1), second).astype(jnp.bfloat16))
        mixed = jnp.concatenate([jnp.concatenate(even, axis=1), jnp.concatenate(odd, axis=1)], axis=0)
        out_ref[group] = jnp.dot(order_ref[...], mixed, preferred_element_type=jnp.float32).astype(jnp.bfloat16)


def arrange_weights(block_tiles):
    _, blocks, fanin, flat = block_tiles.shape
    groups = 4
    depth = fanin * BLK
    tiles = block_tiles.reshape(blocks, fanin, flat)
    return pl.pallas_call(
        functools.partial(arrange_body, groups),
        grid=(blocks // (WIDE * groups),),
        in_specs=[pl.BlockSpec((WIDE * groups, fanin, flat), lambda i: (i, 0, 0))],
        out_specs=pl.BlockSpec((groups, depth, WIDE * BLK), lambda i: (i, 0, 0)),
        out_shape=jax.ShapeDtypeStruct((blocks // WIDE, depth, WIDE * BLK), jnp.bfloat16),
        scratch_shapes=[pltpu.VMEM((depth, depth), jnp.bfloat16)],
        compiler_params=pltpu.CompilerParams(vmem_limit_bytes=24 * MIB),
        cost_estimate=pl.CostEstimate(flops=2 * blocks * depth * depth * BLK, bytes_accessed=4 * blocks * depth * BLK, transcendentals=0),
        name="arrange_weights",
    )(tiles)


def layer_body(groups, parts, place_ref, bias_ref, *refs):
    part_refs, (weight_ref, out_ref, tile_ref, lhs_ref) = refs[:parts], refs[parts:]
    rows, columns = part_refs[0].shape
    per_part = columns // LANES
    turned = parts * per_part
    step = pl.program_id(0)
    fanin = weight_ref.shape[1] // BLK

    @pl.when(step == 0)
    def _():
        for part, ref in enumerate(part_refs):
            for t in range(per_part):
                tile = ref[:, t * LANES:(t + 1) * LANES]
                tile_ref[part * per_part + t] = tile
                tile_ref[turned + part * per_part + t] = jnp.concatenate([tile[:, BLK:], tile[:, :BLK]], axis=1)

    low = lax.broadcasted_iota(jnp.int32, (rows, LANES), 1) < BLK
    bias = bias_ref[0]
    for group in range(groups):
        stacked = []
        for member in range(WIDE):
            base = ((step * groups + group) * WIDE + member) * fanin
            picked = []
            for k in range(0, fanin, 2):
                left = tile_ref[place_ref[base + k]]
                right = tile_ref[place_ref[base + k + 1]]
                picked.append(jnp.where(low, left, right))
            stacked.append(jnp.concatenate(picked, axis=1))
        lhs = jnp.concatenate(stacked, axis=0)
        sums = jnp.dot(lhs, weight_ref[group], preferred_element_type=jnp.float32)
        for pair in range(WIDE // 2):
            lanes = slice(pair * LANES, (pair + 1) * LANES)
            first = sums[2 * pair * rows:(2 * pair + 1) * rows, lanes]
            second = sums[(2 * pair + 1) * rows:(2 * pair + 2) * rows, lanes]
            result = jnp.maximum(jnp.where(low, first, second) + bias, 0.0)
            start = (group * (WIDE // 2) + pair) * LANES
            out_ref[:, start:start + LANES] = result.astype(jnp.bfloat16)


def apply_layer(parts, weights, places, layer_bias):
    rows, columns = parts[0].shape
    total, depth, width = weights.shape
    groups = 4
    tiles = len(parts) * columns // LANES
    whole = pl.BlockSpec((rows, columns), lambda i: (0, 0), pipeline_mode=pl.Buffered(1))
    return pl.pallas_call(
        functools.partial(layer_body, groups, len(parts)),
        grid=(total // groups,),
        in_specs=[pl.BlockSpec(memory_space=pltpu.SMEM), pl.BlockSpec(memory_space=pltpu.SMEM)]
        + [whole] * len(parts)
        + [pl.BlockSpec((groups, depth, width), lambda i: (i, 0, 0))],
        out_specs=pl.BlockSpec((rows, groups * width), lambda i: (0, i)),
        out_shape=jax.ShapeDtypeStruct((rows, total * width), jnp.bfloat16),
        scratch_shapes=[pltpu.VMEM((2 * tiles, rows, LANES), jnp.bfloat16), pltpu.VMEM((WIDE * rows, depth), jnp.bfloat16)],
        compiler_params=pltpu.CompilerParams(vmem_limit_bytes=24 * MIB),
        cost_estimate=pl.CostEstimate(
            flops=2 * rows * total * depth * width,
            bytes_accessed=2 * total * depth * width + 2 * rows * columns * (len(parts) + 1),
            transcendentals=0,
        ),
        name="apply_layer",
    )(places, layer_bias, *parts, weights)


def from_behind(array, axis, by):
    size = lax.axis_size(axis)
    return lax.ppermute(array, axis, [(i, (i + by) % size) for i in range(size)])


def swapped(array, axis, bit):
    return lax.ppermute(array, axis, [(i, i ^ bit) for i in range(lax.axis_size(axis))])


def distances(size):
    held, bit = [0], size // 2
    while bit:
        held, bit = held + [d ^ bit for d in held], bit // 2
    return held


def gather_parts(part):
    held, bit = [part], lax.axis_size("sect") // 2
    while bit:
        held, bit = held + [swapped(h, "sect", bit) for h in held], bit // 2
    return held


def block_places(sources, per_part):
    size = lax.axis_size("sect")
    me = lax.axis_index("sect")
    order = distances(size)
    distance = (sources // per_part) ^ me
    slot = jnp.zeros_like(distance)
    for position, d in enumerate(order):
        slot = jnp.where(distance == d, position, slot)
    inside = sources % per_part
    tile = slot * (per_part // 2) + inside // 2
    position = lax.broadcasted_iota(jnp.int32, sources.shape, sources.ndim - 1)
    return (tile + jnp.where(inside % 2 == position % 2, 0, size * per_part // 2)).reshape(-1)


def per_device(activations, block_tiles, sources, layer_bias):
    places = block_places(sources[0], activations.shape[1] // BLK)
    starts = [sum(CHUNKS[:c]) for c in range(len(CHUNKS))]
    weights = arrange_weights(block_tiles)
    chunks = [activations[s:s + r] for s, r in zip(starts, CHUNKS)]
    for tick in range(2):
        gathered = [gather_parts(chunk) for chunk in chunks]
        hidden = [apply_layer(parts, weights, places, layer_bias) for parts in gathered]
        chunks = [from_behind(h, "phase", 1) for h in hidden]
    return jnp.concatenate(chunks, axis=0)


def solution(mesh):
    in_specs = (
        P("phase", "sect"),
        P("phase", "sect", None, None),
        P("phase", "sect", None),
        P("phase"),
    )
    out_specs = P("phase", "sect")
    return jax.shard_map(
        per_device, mesh=mesh, in_specs=in_specs, out_specs=out_specs, check_vma=False
    )
```

```python
import functools

import jax
import jax.numpy as jnp
from jax import lax
from jax.experimental import pallas as pl
from jax.experimental.pallas import tpu as pltpu
from jax.sharding import PartitionSpec as P

BLK = 64
LANES = 128
WIDE = 4
STREAMS = 4
CHUNKS = (32, 32, 32, 32)
PIECES = 2
TOKEN = (8, LANES)
MIB = 1 << 20
ROOMY = 14 * MIB
TINY = pl.CostEstimate(flops=1, bytes_accessed=1, transcendentals=0)


def arrange_body(*refs):
    tile_refs, out_refs, (token_ref, order_ref) = refs[:STREAMS], refs[STREAMS + 1:2 * STREAMS + 1], refs[2 * STREAMS + 1:]
    fanin = tile_refs[0].shape[1]
    depth = fanin * BLK
    half = depth // 2

    @pl.when(pl.program_id(0) == 0)
    def _():
        row = lax.broadcasted_iota(jnp.int32, (depth, depth), 0)
        column = lax.broadcasted_iota(jnp.int32, (depth, depth), 1)
        neuron = row % BLK
        origin = (neuron % 2) * half + (neuron // 2) * fanin + row // BLK
        order_ref[...] = jnp.where(column == origin, 1.0, 0.0).astype(jnp.bfloat16)
        token_ref[...] = jnp.zeros_like(token_ref)

    low = lax.broadcasted_iota(jnp.int32, (half, LANES), 1) < BLK
    for tiles_ref, out_ref in zip(tile_refs, out_refs):
        stacked = []
        for member in range(WIDE):
            flat = tiles_ref[member].astype(jnp.float32)
            stacked.append(jnp.concatenate([flat[:, t * LANES:(t + 1) * LANES] for t in range(half // fanin)], axis=0))
        even, odd = [], []
        for pair in range(WIDE // 2):
            first, second = stacked[2 * pair], stacked[2 * pair + 1]
            even.append(jnp.where(low, first, pltpu.roll(second, BLK, axis=1)).astype(jnp.bfloat16))
            odd.append(jnp.where(low, pltpu.roll(first, BLK, axis=1), second).astype(jnp.bfloat16))
        mixed = jnp.concatenate([jnp.concatenate(even, axis=1), jnp.concatenate(odd, axis=1)], axis=0)
        out_ref[0] = jnp.dot(order_ref[...], mixed, preferred_element_type=jnp.float32).astype(jnp.bfloat16)


def arrange_weights(block_tiles, earlier):
    _, blocks, fanin, flat = block_tiles.shape
    steps = blocks // (WIDE * STREAMS)
    depth = fanin * BLK
    tiles = block_tiles.reshape(blocks, fanin, flat)
    return pl.pallas_call(
        arrange_body,
        grid=(steps,),
        in_specs=[pl.BlockSpec((WIDE, fanin, flat), lambda i, q=q: (STREAMS * i + q, 0, 0)) for q in range(STREAMS)]
        + [pl.BlockSpec(memory_space=pl.ANY)],
        out_specs=[pl.BlockSpec((1, depth, WIDE * BLK), lambda i: (i, 0, 0))] * STREAMS + [pl.BlockSpec(TOKEN, lambda i: (0, 0))],
        out_shape=[pltpu.VMEM((steps, depth, WIDE * BLK), jnp.bfloat16)] * STREAMS + [jax.ShapeDtypeStruct(TOKEN, jnp.float32)],
        scratch_shapes=[pltpu.VMEM((depth, depth), jnp.bfloat16)],
        compiler_params=pltpu.CompilerParams(vmem_limit_bytes=ROOMY),
        cost_estimate=TINY,
        name="arrange_weights",
    )(*[tiles] * STREAMS, earlier)


def layer_body(parts, waited, place_ref, bias_ref, *refs):
    pieces = sum(parts)
    piece_refs, weight_refs = refs[:pieces], refs[pieces:pieces + STREAMS]
    out_ref, tile_ref = refs[pieces + STREAMS + waited:]
    rows = out_ref.shape[0]
    turned = tile_ref.shape[0] // 2
    step = pl.program_id(0)
    fanin = weight_refs[0].shape[1] // BLK

    @pl.when(step == 0)
    def _():
        place = 0
        for ref in piece_refs:
            for t in range(ref.shape[1] // LANES):
                tile = ref[:, t * LANES:(t + 1) * LANES]
                tile_ref[place] = tile
                tile_ref[turned + place] = jnp.concatenate([tile[:, BLK:], tile[:, :BLK]], axis=1)
                place += 1

    low = lax.broadcasted_iota(jnp.int32, (rows, LANES), 1) < BLK
    bias = bias_ref[0]
    for q, weight_ref in enumerate(weight_refs):
        stacked = []
        for member in range(WIDE):
            base = ((step * STREAMS + q) * WIDE + member) * fanin
            picked = []
            for k in range(0, fanin, 2):
                left = tile_ref[place_ref[base + k]]
                right = tile_ref[place_ref[base + k + 1]]
                picked.append(jnp.where(low, left, right))
            stacked.append(jnp.concatenate(picked, axis=1))
        lhs = jnp.concatenate(stacked, axis=0)
        sums = jnp.dot(lhs, weight_ref[0], preferred_element_type=jnp.float32)
        for pair in range(WIDE // 2):
            lanes = slice(pair * LANES, (pair + 1) * LANES)
            first = sums[2 * pair * rows:(2 * pair + 1) * rows, lanes]
            second = sums[(2 * pair + 1) * rows:(2 * pair + 2) * rows, lanes]
            result = jnp.maximum(jnp.where(low, first, second) + bias, 0.0)
            start = (q * (WIDE // 2) + pair) * LANES
            out_ref[:, start:start + LANES] = result.astype(jnp.bfloat16)


def apply_layer(rows, parts, weights, places, layer_bias, earlier):
    pieces = [piece for part in parts for piece in part]
    columns = sum(array.shape[1] for array, _ in pieces)
    steps, depth, width = weights[0].shape
    in_specs = [pl.BlockSpec(memory_space=pltpu.SMEM), pl.BlockSpec(memory_space=pltpu.SMEM)]
    for array, block in pieces:
        in_specs.append(pl.BlockSpec((rows, array.shape[1]), lambda i, block=block: (block, 0), pipeline_mode=pl.Buffered(1)))
    in_specs += [pl.BlockSpec((1, depth, width), lambda i: (i, 0, 0))] * STREAMS
    in_specs += [pl.BlockSpec(memory_space=pl.ANY)] * len(earlier)
    return pl.pallas_call(
        functools.partial(layer_body, [len(part) for part in parts], len(earlier)),
        grid=(steps,),
        in_specs=in_specs,
        out_specs=pl.BlockSpec((rows, STREAMS * width), lambda i: (0, i)),
        out_shape=jax.ShapeDtypeStruct((rows, steps * STREAMS * width), jnp.bfloat16),
        scratch_shapes=[pltpu.VMEM((2 * columns // LANES, rows, LANES), jnp.bfloat16)],
        compiler_params=pltpu.CompilerParams(vmem_limit_bytes=ROOMY),
        cost_estimate=TINY,
        name="apply_layer",
    )(places, layer_bias, *[array for array, _ in pieces], *weights, *earlier)


def from_behind(array, axis, by):
    size = lax.axis_size(axis)
    return lax.ppermute(array, axis, [(i, (i + by) % size) for i in range(size)])


def swapped(array, axis, bit):
    return lax.ppermute(array, axis, [(i, i ^ bit) for i in range(lax.axis_size(axis))])


def distances(size):
    held, bit = [0], size // 2
    while bit:
        held, bit = held + [d ^ bit for d in held], bit // 2
    return held


def block_places(sources, per_part):
    size = lax.axis_size("sect")
    me = lax.axis_index("sect")
    order = distances(size)
    distance = (sources // per_part) ^ me
    slot = jnp.zeros_like(distance)
    for position, d in enumerate(order):
        slot = jnp.where(distance == d, position, slot)
    inside = sources % per_part
    tile = slot * (per_part // 2) + inside // 2
    position = lax.broadcasted_iota(jnp.int32, sources.shape, sources.ndim - 1)
    return (tile + jnp.where(inside % 2 == position % 2, 0, size * per_part // 2)).reshape(-1)


def nothing(*refs):
    del refs


def tie(array, *earlier):
    anywhere = pl.BlockSpec(memory_space=pl.ANY)
    return pl.pallas_call(
        nothing,
        in_specs=[anywhere] * (1 + len(earlier)),
        out_specs=anywhere,
        out_shape=jax.ShapeDtypeStruct(array.shape, array.dtype),
        input_output_aliases={0: 0},
        compiler_params=pltpu.CompilerParams(vmem_limit_bytes=MIB),
        cost_estimate=TINY,
        name="tie",
    )(array, *earlier)


def per_device(activations, block_tiles, sources, layer_bias):
    places = block_places(sources[0], activations.shape[1] // BLK)
    count = len(CHUNKS)
    starts = [sum(CHUNKS[:c]) for c in range(count)]
    size = lax.axis_size("sect")
    top, rest = size // 2, size // 4

    state = [activations[s:s + r] for s, r in zip(starts, CHUNKS)]
    far = [swapped(chunk, "sect", top) for chunk in state]
    near = swapped(activations, "sect", rest)
    *weights, token = arrange_weights(block_tiles, places)
    relayed, far_next, near_next, result = {}, {}, {}, {}
    latest = []

    def layer(c, own, far_part, near_part, pins):
        far_part = tie(far_part, *(latest[-1:] or [token]))
        pieces = PIECES if latest else 1
        wide = far_part.shape[1] // pieces
        across = [(swapped(far_part[:, p * wide:(p + 1) * wide], "sect", rest), 0) for p in range(pieces)]
        hidden = apply_layer(CHUNKS[c], [[own], [(far_part, 0)], [near_part], across], weights, places, layer_bias, latest[-1:] + pins)
        latest.append(hidden)
        return from_behind(hidden, "phase", 1)

    def first(c, pins):
        block = starts[c] // CHUNKS[c]
        relayed[c] = layer(c, (activations, block), far[c], (near, block), pins)

    def spread(c):
        relayed[c] = tie(relayed[c], latest[-1])
        far_next[c] = swapped(relayed[c], "sect", top)
        near_next[c] = swapped(relayed[c], "sect", rest)

    def second(c, pins):
        result[c] = layer(c, (relayed[c], 0), far_next[c], (near_next[c], 0), pins)

    first(0, [])
    for c in range(1, count):
        first(c, [near_next[c - 2]] if c > 1 else [])
        spread(c - 1)
    second(0, [near_next[count - 2]])
    spread(count - 1)
    for c in range(1, count):
        second(c, [near_next[count - 1]] if c == 1 else [result[c - 2]])
    return jnp.concatenate([result[c] for c in range(count)], axis=0)


def solution(mesh):
    in_specs = (
        P("phase", "sect"),
        P("phase", "sect", None, None),
        P("phase", "sect", None),
        P("phase"),
    )
    out_specs = P("phase", "sect")
    return jax.shard_map(
        per_device, mesh=mesh, in_specs=in_specs, out_specs=out_specs, check_vma=False
    )
```

```python
import functools

import jax
import jax.numpy as jnp
from jax import lax
from jax.experimental import pallas as pl
from jax.experimental.pallas import tpu as pltpu
from jax.sharding import PartitionSpec as P

BLK = 64
LANES = 128
WIDE = 4
STREAMS = 4
CHUNKS = (32, 32, 32, 32)
PIECES = 2
TICKS = 2
TOKEN = (8, LANES)
MIB = 1 << 20
ROOMY = 14 * MIB
TINY = pl.CostEstimate(flops=1, bytes_accessed=1, transcendentals=0)
SOME = pl.CostEstimate(flops=4 << 30, bytes_accessed=1, transcendentals=0)


def arrange_body(*refs):
    tile_refs, out_refs, (token_ref, order_ref) = refs[:STREAMS], refs[STREAMS + 1:2 * STREAMS + 1], refs[2 * STREAMS + 1:]
    fanin = tile_refs[0].shape[1]
    depth = fanin * BLK
    half = depth // 2

    @pl.when(pl.program_id(0) == 0)
    def _():
        row = lax.broadcasted_iota(jnp.int32, (depth, depth), 0)
        column = lax.broadcasted_iota(jnp.int32, (depth, depth), 1)
        neuron = row % BLK
        origin = (neuron % 2) * half + (neuron // 2) * fanin + row // BLK
        order_ref[...] = jnp.where(column == origin, 1.0, 0.0).astype(jnp.bfloat16)
        token_ref[...] = jnp.zeros_like(token_ref)

    low = lax.broadcasted_iota(jnp.int32, (half, LANES), 1) < BLK
    for tiles_ref, out_ref in zip(tile_refs, out_refs):
        stacked = []
        for member in range(WIDE):
            flat = tiles_ref[member].astype(jnp.float32)
            stacked.append(jnp.concatenate([flat[:, t * LANES:(t + 1) * LANES] for t in range(half // fanin)], axis=0))
        even, odd = [], []
        for pair in range(WIDE // 2):
            first, second = stacked[2 * pair], stacked[2 * pair + 1]
            even.append(jnp.where(low, first, pltpu.roll(second, BLK, axis=1)).astype(jnp.bfloat16))
            odd.append(jnp.where(low, pltpu.roll(first, BLK, axis=1), second).astype(jnp.bfloat16))
        mixed = jnp.concatenate([jnp.concatenate(even, axis=1), jnp.concatenate(odd, axis=1)], axis=0)
        out_ref[0] = jnp.dot(order_ref[...], mixed, preferred_element_type=jnp.float32).astype(jnp.bfloat16)


def arrange_weights(block_tiles, earlier):
    _, blocks, fanin, flat = block_tiles.shape
    steps = blocks // (WIDE * STREAMS)
    depth = fanin * BLK
    tiles = block_tiles.reshape(blocks, fanin, flat)
    return pl.pallas_call(
        arrange_body,
        grid=(steps,),
        in_specs=[pl.BlockSpec((WIDE, fanin, flat), lambda i, q=q: (STREAMS * i + q, 0, 0)) for q in range(STREAMS)]
        + [pl.BlockSpec(memory_space=pl.ANY)],
        out_specs=[pl.BlockSpec((1, depth, WIDE * BLK), lambda i: (i, 0, 0))] * STREAMS + [pl.BlockSpec(TOKEN, lambda i: (0, 0))],
        out_shape=[pltpu.VMEM((steps, depth, WIDE * BLK), jnp.bfloat16)] * STREAMS + [jax.ShapeDtypeStruct(TOKEN, jnp.float32)],
        scratch_shapes=[pltpu.VMEM((depth, depth), jnp.bfloat16)],
        compiler_params=pltpu.CompilerParams(vmem_limit_bytes=ROOMY),
        cost_estimate=TINY,
        name="arrange_weights",
    )(*[tiles] * STREAMS, earlier)


def layer_body(parts, waited, place_ref, bias_ref, *refs):
    pieces = sum(parts)
    piece_refs, weight_refs = refs[:pieces], refs[pieces:pieces + STREAMS]
    out_ref, tile_ref = refs[pieces + STREAMS + waited:]
    rows = out_ref.shape[0]
    turned = tile_ref.shape[0] // 2
    step = pl.program_id(0)
    fanin = weight_refs[0].shape[1] // BLK

    @pl.when(step == 0)
    def _():
        place = 0
        for ref in piece_refs:
            for t in range(ref.shape[1] // LANES):
                tile = ref[:, t * LANES:(t + 1) * LANES]
                tile_ref[place] = tile
                tile_ref[turned + place] = jnp.concatenate([tile[:, BLK:], tile[:, :BLK]], axis=1)
                place += 1

    low = lax.broadcasted_iota(jnp.int32, (rows, LANES), 1) < BLK
    bias = bias_ref[0]
    for q, weight_ref in enumerate(weight_refs):
        stacked = []
        for member in range(WIDE):
            base = ((step * STREAMS + q) * WIDE + member) * fanin
            picked = []
            for k in range(0, fanin, 2):
                left = tile_ref[place_ref[base + k]]
                right = tile_ref[place_ref[base + k + 1]]
                picked.append(jnp.where(low, left, right))
            stacked.append(jnp.concatenate(picked, axis=1))
        lhs = jnp.concatenate(stacked, axis=0)
        sums = jnp.dot(lhs, weight_ref[0], preferred_element_type=jnp.float32)
        for pair in range(WIDE // 2):
            lanes = slice(pair * LANES, (pair + 1) * LANES)
            first = sums[2 * pair * rows:(2 * pair + 1) * rows, lanes]
            second = sums[(2 * pair + 1) * rows:(2 * pair + 2) * rows, lanes]
            result = jnp.maximum(jnp.where(low, first, second) + bias, 0.0)
            start = (q * (WIDE // 2) + pair) * LANES
            out_ref[:, start:start + LANES] = result.astype(jnp.bfloat16)


def apply_layer(rows, parts, weights, places, layer_bias, earlier):
    pieces = [piece for part in parts for piece in part]
    columns = sum(array.shape[1] for array, _ in pieces)
    steps, depth, width = weights[0].shape
    in_specs = [pl.BlockSpec(memory_space=pltpu.SMEM), pl.BlockSpec(memory_space=pltpu.SMEM)]
    for array, block in pieces:
        in_specs.append(pl.BlockSpec((rows, array.shape[1]), lambda i, block=block: (block, 0), pipeline_mode=pl.Buffered(1)))
    in_specs += [pl.BlockSpec((1, depth, width), lambda i: (i, 0, 0))] * STREAMS
    in_specs += [pl.BlockSpec(memory_space=pl.ANY)] * len(earlier)
    return pl.pallas_call(
        functools.partial(layer_body, [len(part) for part in parts], len(earlier)),
        grid=(steps,),
        in_specs=in_specs,
        out_specs=pl.BlockSpec((rows, STREAMS * width), lambda i: (0, i)),
        out_shape=jax.ShapeDtypeStruct((rows, steps * STREAMS * width), jnp.bfloat16),
        scratch_shapes=[pltpu.VMEM((2 * columns // LANES, rows, LANES), jnp.bfloat16)],
        compiler_params=pltpu.CompilerParams(vmem_limit_bytes=ROOMY),
        cost_estimate=TINY,
        name="apply_layer",
    )(places, layer_bias, *[array for array, _ in pieces], *weights, *earlier)


def from_behind(array, axis, by):
    size = lax.axis_size(axis)
    return lax.ppermute(array, axis, [(i, (i + by) % size) for i in range(size)])


def swapped(array, axis, bit):
    return lax.ppermute(array, axis, [(i, i ^ bit) for i in range(lax.axis_size(axis))])


def distances(size):
    held, bit = [0], size // 2
    while bit:
        held, bit = held + [d ^ bit for d in held], bit // 2
    return held


def block_places(sources, per_part):
    size = lax.axis_size("sect")
    me = lax.axis_index("sect")
    order = distances(size)
    distance = (sources // per_part) ^ me
    slot = jnp.zeros_like(distance)
    for position, d in enumerate(order):
        slot = jnp.where(distance == d, position, slot)
    inside = sources % per_part
    tile = slot * (per_part // 2) + inside // 2
    position = lax.broadcasted_iota(jnp.int32, sources.shape, sources.ndim - 1)
    return (tile + jnp.where(inside % 2 == position % 2, 0, size * per_part // 2)).reshape(-1)


def copy_body(array_ref, *refs):
    refs[-1][...] = array_ref[...]


def row_block(array, block, rows, earlier):
    columns = array.shape[1]
    return pl.pallas_call(
        copy_body,
        grid=(1,),
        in_specs=[pl.BlockSpec((rows, columns), lambda i: (block, 0))] + [pl.BlockSpec(memory_space=pl.ANY)] * len(earlier),
        out_specs=pl.BlockSpec((rows, columns), lambda i: (0, 0)),
        out_shape=jax.ShapeDtypeStruct((rows, columns), array.dtype),
        compiler_params=pltpu.CompilerParams(vmem_limit_bytes=4 * MIB),
        cost_estimate=TINY,
        name="row_block",
    )(array, *earlier)


def put_body(start, *refs):
    chunk_ref, out_ref, sem = refs[0], refs[-2], refs[-1]
    copy = pltpu.make_async_copy(chunk_ref, out_ref.at[pl.ds(start, chunk_ref.shape[0])], sem)
    copy.start()
    copy.wait()


def put_rows(chunk, start, total, whole):
    anywhere = pl.BlockSpec(memory_space=pl.ANY)
    operands = [chunk] if whole is None else [chunk, whole]
    return pl.pallas_call(
        functools.partial(put_body, start),
        in_specs=[anywhere] * len(operands),
        out_specs=anywhere,
        out_shape=jax.ShapeDtypeStruct((total, chunk.shape[1]), chunk.dtype),
        input_output_aliases={} if whole is None else {1: 0},
        scratch_shapes=[pltpu.SemaphoreType.DMA],
        compiler_params=pltpu.CompilerParams(vmem_limit_bytes=MIB),
        cost_estimate=TINY,
        name="put_rows",
    )(*operands)


def nothing(*refs):
    del refs


def tie(array, *earlier, cost=TINY):
    anywhere = pl.BlockSpec(memory_space=pl.ANY)
    return pl.pallas_call(
        nothing,
        in_specs=[anywhere] * (1 + len(earlier)),
        out_specs=anywhere,
        out_shape=jax.ShapeDtypeStruct(array.shape, array.dtype),
        input_output_aliases={0: 0},
        compiler_params=pltpu.CompilerParams(vmem_limit_bytes=MIB),
        cost_estimate=cost,
        name="tie",
    )(array, *earlier)


def per_device(activations, block_tiles, sources, layer_bias):
    places = block_places(sources[0], activations.shape[1] // BLK)
    count = len(CHUNKS)
    starts = [sum(CHUNKS[:c]) for c in range(count)]
    size = lax.axis_size("sect")
    top, rest = size // 2, size // 4
    calls, moved, own, far, near = [], [], [], [], []

    near_first = swapped(activations, "sect", rest)
    *weights, token = arrange_weights(block_tiles, places)

    def send(n):
        rows, start = CHUNKS[n % count], starts[n % count]
        if n < count:
            chunk = row_block(activations, start // rows, rows, [token] if n == 1 else [])
            own.append((activations, start // rows))
            near.append((near_first, start // rows))
        else:
            chunk = tie(moved[n - count], calls[n - 2])
            own.append((chunk, 0))
            near.append((swapped(chunk, "sect", rest), 0))
        far.append(swapped(chunk, "sect", top))

    send(0)
    send(1)
    for n in range(TICKS * count):
        here = tie(far[n], *(calls[-1:] or [token]), *moved[max(0, n - 2):max(0, n - 1)])
        wide = here.shape[1] // PIECES
        across = [(swapped(here[:, p * wide:(p + 1) * wide], "sect", rest), 0) for p in range(PIECES)]
        parts = [[own[n]], [(here, 0)], [near[n]], across]
        calls.append(apply_layer(CHUNKS[n % count], parts, weights, places, layer_bias, calls[-1:]))
        moved.append(from_behind(calls[n], "phase", 1))
        if n + 2 < TICKS * count:
            send(n + 2)
    moved[-2] = tie(moved[-2], cost=SOME)
    return jnp.concatenate(moved[-count:], axis=0)


def solution(mesh):
    in_specs = (
        P("phase", "sect"),
        P("phase", "sect", None, None),
        P("phase", "sect", None),
        P("phase"),
    )
    out_specs = P("phase", "sect")
    return jax.shard_map(
        per_device, mesh=mesh, in_specs=in_specs, out_specs=out_specs, check_vma=False
    )
```

```python
import functools

import jax
import jax.numpy as jnp
from jax import lax
from jax.experimental import pallas as pl
from jax.experimental.pallas import tpu as pltpu
from jax.sharding import PartitionSpec as P

BLK = 64
LANES = 128
WIDE = 4
STREAMS = 4
CHUNKS = (32, 32, 32, 32)
PIECES = 2
TICKS = 2
TOKEN = (8, LANES)
MIB = 1 << 20
ROOMY = 14 * MIB
TINY = pl.CostEstimate(flops=1, bytes_accessed=1, transcendentals=0)
SOME = pl.CostEstimate(flops=4 << 30, bytes_accessed=1, transcendentals=0)


def arrange_body(*refs):
    tile_refs, out_refs, (token_ref, order_ref) = refs[:STREAMS], refs[STREAMS + 1:2 * STREAMS + 1], refs[2 * STREAMS + 1:]
    fanin = tile_refs[0].shape[1]
    depth = fanin * BLK
    half = depth // 2

    @pl.when(pl.program_id(0) == 0)
    def _():
        row = lax.broadcasted_iota(jnp.int32, (depth, depth), 0)
        column = lax.broadcasted_iota(jnp.int32, (depth, depth), 1)
        neuron = row % BLK
        origin = (neuron % 2) * half + (neuron // 2) * fanin + row // BLK
        order_ref[...] = jnp.where(column == origin, 1.0, 0.0).astype(jnp.bfloat16)
        token_ref[...] = jnp.zeros_like(token_ref)

    low = lax.broadcasted_iota(jnp.int32, (half, LANES), 1) < BLK
    for tiles_ref, out_ref in zip(tile_refs, out_refs):
        stacked = []
        for member in range(WIDE):
            flat = tiles_ref[member].astype(jnp.float32)
            stacked.append(jnp.concatenate([flat[:, t * LANES:(t + 1) * LANES] for t in range(half // fanin)], axis=0))
        even, odd = [], []
        for pair in range(WIDE // 2):
            first, second = stacked[2 * pair], stacked[2 * pair + 1]
            even.append(jnp.where(low, first, pltpu.roll(second, BLK, axis=1)).astype(jnp.bfloat16))
            odd.append(jnp.where(low, pltpu.roll(first, BLK, axis=1), second).astype(jnp.bfloat16))
        mixed = jnp.concatenate([jnp.concatenate(even, axis=1), jnp.concatenate(odd, axis=1)], axis=0)
        out_ref[0] = jnp.dot(order_ref[...], mixed, preferred_element_type=jnp.float32).astype(jnp.bfloat16)


def arrange_weights(block_tiles, earlier):
    _, blocks, fanin, flat = block_tiles.shape
    steps = blocks // (WIDE * STREAMS)
    depth = fanin * BLK
    tiles = block_tiles.reshape(blocks, fanin, flat)
    return pl.pallas_call(
        arrange_body,
        grid=(steps,),
        in_specs=[pl.BlockSpec((WIDE, fanin, flat), lambda i, q=q: (STREAMS * i + q, 0, 0)) for q in range(STREAMS)]
        + [pl.BlockSpec(memory_space=pl.ANY)],
        out_specs=[pl.BlockSpec((1, depth, WIDE * BLK), lambda i: (i, 0, 0))] * STREAMS + [pl.BlockSpec(TOKEN, lambda i: (0, 0))],
        out_shape=[pltpu.VMEM((steps, depth, WIDE * BLK), jnp.bfloat16)] * STREAMS + [jax.ShapeDtypeStruct(TOKEN, jnp.float32)],
        scratch_shapes=[pltpu.VMEM((depth, depth), jnp.bfloat16)],
        compiler_params=pltpu.CompilerParams(vmem_limit_bytes=ROOMY),
        cost_estimate=TINY,
        name="arrange_weights",
    )(*[tiles] * STREAMS, earlier)


def layer_body(pieces, waited, place_ref, bias_ref, *refs):
    piece_refs, weight_refs = refs[:pieces], refs[pieces:pieces + STREAMS]
    out_ref, tile_ref = refs[pieces + STREAMS + waited:]
    rows = out_ref.shape[0]
    turned = tile_ref.shape[0] // 2
    steps, depth, width = weight_refs[0].shape
    fanin = depth // BLK

    place = 0
    for ref in piece_refs:
        for t in range(ref.shape[1] // LANES):
            tile = ref[:, t * LANES:(t + 1) * LANES]
            tile_ref[place] = tile
            tile_ref[turned + place] = jnp.concatenate([tile[:, BLK:], tile[:, :BLK]], axis=1)
            place += 1

    low = lax.broadcasted_iota(jnp.int32, (rows, LANES), 1) < BLK
    bias = bias_ref[0]

    @pl.loop(0, steps, unroll=steps)
    def _(step):
        for q, weight_ref in enumerate(weight_refs):
            stacked = []
            for member in range(WIDE):
                base = ((step * STREAMS + q) * WIDE + member) * fanin
                picked = []
                for k in range(0, fanin, 2):
                    left = tile_ref[place_ref[base + k]]
                    right = tile_ref[place_ref[base + k + 1]]
                    picked.append(jnp.where(low, left, right))
                stacked.append(jnp.concatenate(picked, axis=1))
            lhs = jnp.concatenate(stacked, axis=0)
            sums = jnp.dot(lhs, weight_ref[step], preferred_element_type=jnp.float32)
            for pair in range(WIDE // 2):
                lanes = slice(pair * LANES, (pair + 1) * LANES)
                first = sums[2 * pair * rows:(2 * pair + 1) * rows, lanes]
                second = sums[(2 * pair + 1) * rows:(2 * pair + 2) * rows, lanes]
                result = jnp.maximum(jnp.where(low, first, second) + bias, 0.0)
                start = pl.multiple_of((step * STREAMS + q) * width + pair * LANES, LANES)
                out_ref[:, pl.ds(start, LANES)] = result.astype(jnp.bfloat16)


def apply_layer(rows, parts, weights, places, layer_bias, earlier):
    pieces = [piece for part in parts for piece in part]
    columns = sum(array.shape[1] for array, _ in pieces)
    steps, depth, width = weights[0].shape
    in_specs = [pl.BlockSpec(memory_space=pltpu.SMEM), pl.BlockSpec(memory_space=pltpu.SMEM)]
    for array, block in pieces:
        if array.shape[0] == rows:
            in_specs.append(pl.BlockSpec(memory_space=pltpu.VMEM))
        else:
            in_specs.append(pl.BlockSpec((rows, array.shape[1]), lambda i, block=block: (block, 0), pipeline_mode=pl.Buffered(1)))
    in_specs += [pl.BlockSpec(memory_space=pltpu.VMEM)] * STREAMS
    in_specs += [pl.BlockSpec(memory_space=pl.ANY)] * len(earlier)
    return pl.pallas_call(
        functools.partial(layer_body, len(pieces), len(earlier)),
        grid=(1,),
        in_specs=in_specs,
        out_specs=pl.BlockSpec(memory_space=pltpu.VMEM),
        out_shape=jax.ShapeDtypeStruct((rows, steps * STREAMS * width), jnp.bfloat16),
        scratch_shapes=[pltpu.VMEM((2 * columns // LANES, rows, LANES), jnp.bfloat16)],
        compiler_params=pltpu.CompilerParams(vmem_limit_bytes=24 * MIB),
        cost_estimate=TINY,
        name="apply_layer",
    )(places, layer_bias, *[array for array, _ in pieces], *weights, *earlier)


def from_behind(array, axis, by):
    size = lax.axis_size(axis)
    return lax.ppermute(array, axis, [(i, (i + by) % size) for i in range(size)])


def swapped(array, axis, bit):
    return lax.ppermute(array, axis, [(i, i ^ bit) for i in range(lax.axis_size(axis))])


def distances(size):
    held, bit = [0], size // 2
    while bit:
        held, bit = held + [d ^ bit for d in held], bit // 2
    return held


def block_places(sources, per_part):
    size = lax.axis_size("sect")
    me = lax.axis_index("sect")
    order = distances(size)
    distance = (sources // per_part) ^ me
    slot = jnp.zeros_like(distance)
    for position, d in enumerate(order):
        slot = jnp.where(distance == d, position, slot)
    inside = sources % per_part
    tile = slot * (per_part // 2) + inside // 2
    position = lax.broadcasted_iota(jnp.int32, sources.shape, sources.ndim - 1)
    return (tile + jnp.where(inside % 2 == position % 2, 0, size * per_part // 2)).reshape(-1)


def copy_body(array_ref, *refs):
    refs[-1][...] = array_ref[...]


def row_block(array, block, rows, earlier):
    columns = array.shape[1]
    return pl.pallas_call(
        copy_body,
        grid=(1,),
        in_specs=[pl.BlockSpec((rows, columns), lambda i: (block, 0))] + [pl.BlockSpec(memory_space=pl.ANY)] * len(earlier),
        out_specs=pl.BlockSpec((rows, columns), lambda i: (0, 0)),
        out_shape=jax.ShapeDtypeStruct((rows, columns), array.dtype),
        compiler_params=pltpu.CompilerParams(vmem_limit_bytes=4 * MIB),
        cost_estimate=TINY,
        name="row_block",
    )(array, *earlier)


def put_body(start, *refs):
    chunk_ref, out_ref, sem = refs[0], refs[-2], refs[-1]
    copy = pltpu.make_async_copy(chunk_ref, out_ref.at[pl.ds(start, chunk_ref.shape[0])], sem)
    copy.start()
    copy.wait()


def put_rows(chunk, start, total, whole):
    anywhere = pl.BlockSpec(memory_space=pl.ANY)
    operands = [chunk] if whole is None else [chunk, whole]
    return pl.pallas_call(
        functools.partial(put_body, start),
        in_specs=[anywhere] * len(operands),
        out_specs=anywhere,
        out_shape=jax.ShapeDtypeStruct((total, chunk.shape[1]), chunk.dtype),
        input_output_aliases={} if whole is None else {1: 0},
        scratch_shapes=[pltpu.SemaphoreType.DMA],
        compiler_params=pltpu.CompilerParams(vmem_limit_bytes=MIB),
        cost_estimate=TINY,
        name="put_rows",
    )(*operands)


def nothing(*refs):
    del refs


def tie(array, *earlier, cost=TINY):
    anywhere = pl.BlockSpec(memory_space=pl.ANY)
    return pl.pallas_call(
        nothing,
        in_specs=[anywhere] * (1 + len(earlier)),
        out_specs=anywhere,
        out_shape=jax.ShapeDtypeStruct(array.shape, array.dtype),
        input_output_aliases={0: 0},
        compiler_params=pltpu.CompilerParams(vmem_limit_bytes=MIB),
        cost_estimate=cost,
        name="tie",
    )(array, *earlier)


def per_device(activations, block_tiles, sources, layer_bias):
    places = block_places(sources[0], activations.shape[1] // BLK)
    count = len(CHUNKS)
    starts = [sum(CHUNKS[:c]) for c in range(count)]
    size = lax.axis_size("sect")
    top, rest = size // 2, size // 4
    calls, moved, own, far, near = [], [], [], [], []

    near_first = swapped(activations, "sect", rest)
    *weights, token = arrange_weights(block_tiles, places)

    def send(n):
        rows, start = CHUNKS[n % count], starts[n % count]
        if n < count:
            chunk = row_block(activations, start // rows, rows, [token] if n == 1 else [])
            own.append((chunk, 0))
            near.append((near_first, start // rows))
        else:
            chunk = tie(moved[n - count], calls[n - 2])
            own.append((chunk, 0))
            near.append((swapped(chunk, "sect", rest), 0))
        far.append(swapped(chunk, "sect", top))

    send(0)
    send(1)
    for n in range(TICKS * count):
        here = tie(far[n], *(calls[-1:] or [token]), *moved[max(0, n - 2):max(0, n - 1)])
        wide = here.shape[1] // PIECES
        across = [(swapped(here[:, p * wide:(p + 1) * wide], "sect", rest), 0) for p in range(PIECES)]
        parts = [[own[n]], [(here, 0)], [near[n]], across]
        calls.append(apply_layer(CHUNKS[n % count], parts, weights, places, layer_bias, calls[-1:]))
        moved.append(from_behind(calls[n], "phase", 1))
        if n + 2 < TICKS * count:
            send(n + 2)
    moved[-2] = tie(moved[-2], cost=SOME)
    whole = None
    for c in range(count):
        whole = put_rows(moved[c - count], starts[c], activations.shape[0], whole)
    return whole


def solution(mesh):
    in_specs = (
        P("phase", "sect"),
        P("phase", "sect", None, None),
        P("phase", "sect", None),
        P("phase"),
    )
    out_specs = P("phase", "sect")
    return jax.shard_map(
        per_device, mesh=mesh, in_specs=in_specs, out_specs=out_specs, check_vma=False
    )
```
